32 devices in a mesh: row: 16 (over z, x, core), col: 2 (over y).
Axes of the slice: x: 2, y: 2, z: 4, core: 2. Of those that a mesh axis runs over, the one named last changes fastest.
Arguments:
- trailing: float32 [8192, 2048], P('row', 'col'), may hold values from -6 to 6
- reflectors: float32 [8192, 256], P('row', 'col'), may hold values from -0.25 to 0.25
- leaf_factor: float32 [4096, 256], P('row', 'col'), may hold values from -0.5 to 0.5
- node_reflect: float32 [4, 4096, 256], P(None, 'row', 'col'), may hold values from -0.375 to 0.375
- node_factor: float32 [4, 4096, 256], P(None, 'row', 'col'), may hold values from -0.5 to 0.5
Outputs:
- updated: float32 [8192, 2048], P('row', 'col')
The draws below stay inside these ranges and needn't reach their ends.
All inputs are finite; a program needn't handle non-finite values.
Results may differ from the reference program's by a relative error of at most 0.00014.
Values sent between devices are 32-bit elements; how exact they have to be, the bound alone decides.
No kernel may reach another device: no remote copies, remote signals or barrier semaphores. Data moves between devices by JAX's collectives and lax.ppermute only.
A program may use at most 64 MiB of HBM per device.

```python
import jax
import jax.numpy as jnp
from jax import lax

B = 256
ROWS_DEV = 512
ROWS = 8192
COLS = 2048
SECTIONS = 4
N_ROW = 16


def block_levels(key, shape, pieces, low, largest):
    def one(axis_at, shards_of):
        draws = jax.random.uniform(jax.random.fold_in(jax.random.fold_in(key, 6), axis_at), (shards_of,), jnp.float32, low / len(pieces), largest / len(pieces))
        return jnp.repeat(jnp.exp(draws), shape[axis_at] // shards_of).reshape((-1,) + (1,) * (len(shape) - axis_at - 1))

    level = one(*pieces[0])
    for cut in pieces[1:]:
        level = level * one(*cut)
    return level


def bell_draw(own_key, extent, scale, most, pieces=(), held_as=jnp.bfloat16):
    gain = block_levels(own_key, extent, pieces, -0.22, 0.18) if pieces else 1.0
    values = jax.random.normal(own_key, extent, jnp.float32) * scale * gain
    return jnp.minimum(jnp.maximum(values, -most), most).astype(held_as)


def setup_inputs(seed: int = 0) -> dict:
    splits = jax.random.split(jax.random.key(seed), 6)
    trailing = bell_draw(splits[0], (ROWS, COLS), 1.0, 6.0, ((0, 16), (1, 2)), jnp.float32)
    reflectors = bell_draw(splits[1], (ROWS, B), ROWS_DEV ** -0.5, 0.25, ((0, 16), (1, 2)), jnp.float32)
    leaf_factor = bell_draw(splits[2], (N_ROW * B, B), (0.5 / B ** 0.5), 0.5, ((0, 16), (1, 2)), jnp.float32)
    node_reflect = bell_draw(splits[3], (SECTIONS, N_ROW * B, B), B ** -0.5, 0.375, ((1, 16), (2, 2)), jnp.float32)
    node_factor = bell_draw(splits[4], (SECTIONS, N_ROW * B, B), (0.5 / B ** 0.5), 0.5, ((1, 16), (2, 2)), jnp.float32)
    return {"trailing": trailing, "reflectors": reflectors, "leaf_factor": leaf_factor, "node_reflect": node_reflect, "node_factor": node_factor}


highest = lax.Precision.HIGHEST


def triangle(factor):
    return jnp.triu(factor) + 0.5 * jnp.eye(factor.shape[-1], dtype=factor.dtype)


def reference(trailing, reflectors, leaf_factor, node_reflect, node_factor):
    width = trailing.shape[1]
    matrix = trailing.reshape(N_ROW, ROWS_DEV, width)
    vectors = reflectors.reshape(N_ROW, ROWS_DEV, B)
    leaf_tri = triangle(leaf_factor.reshape(N_ROW, B, B))
    inner = jnp.einsum("nrb,nrc->nbc", vectors, matrix, precision=highest)
    scaled = jnp.einsum("nkb,nkc->nbc", leaf_tri, inner, precision=highest)
    matrix = matrix - jnp.einsum("nrb,nbc->nrc", vectors, scaled, precision=highest)
    uppers = matrix[:, :B]
    remainder = matrix[:, B:]
    for section in range(SECTIONS):
        offset = 2 ** section
        groups = N_ROW // (2 * offset)
        node_y = node_reflect[section].reshape(groups, 2, offset, B, B)[:, 1]
        node_tri = triangle(node_factor[section].reshape(groups, 2, offset, B, B)[:, 0])
        grouped = uppers.reshape(groups, 2, offset, B, width)
        leaders = grouped[:, 0]
        partners = grouped[:, 1]
        summed = leaders + jnp.einsum("gokb,gokc->gobc", node_y, partners, precision=highest)
        coupling = jnp.einsum("gokb,gokc->gobc", node_tri, summed, precision=highest)
        leaders = leaders - coupling
        partners = partners - jnp.einsum("gobk,gokc->gobc", node_y, coupling, precision=highest)
        uppers = jnp.stack([leaders, partners], axis=1).reshape(N_ROW, B, width)
    result = jnp.concatenate([uppers, remainder], axis=1)
    return result.reshape(N_ROW * ROWS_DEV, width)
```

```python
import functools

import jax
import jax.numpy as jnp
from jax import lax
from jax.experimental import pallas as pl
from jax.experimental.pallas import tpu as pltpu
from jax.sharding import PartitionSpec as P

f32 = jnp.float32
LANES = 128
VMEM_LIMIT = 24 * 2**20


def swapped(value, axis, apart):
    mask = 2**apart
    pairs = [(source, source ^ mask) for source in range(lax.axis_size(axis))]
    return lax.ppermute(value, axis, pairs)


def turned(value, axis):
    size = lax.axis_size(axis)
    return [
        lax.ppermute(value, axis, [((to + step) % size, to) for to in range(size)])
        for step in range(1, size)
    ]


def col_blocks(value):
    if value.shape[-1] % LANES == 0:
        return [value] + turned(value, "col")
    return [lax.all_gather(value, "col", axis=value.ndim - 1, tiled=True)]


def in_vmem(value):
    return pltpu.with_memory_space_constraint(value, pltpu.VMEM)


def whole(blocks):
    if len(blocks) == 1:
        return blocks[0]
    size = len(blocks)
    me = lax.axis_index("col")
    ordered = []
    for at in range(size):
        block = blocks[0]
        for step in range(1, size):
            block = jnp.where((me + step) % size == at, blocks[step], block)
        ordered.append(block)
    return jnp.concatenate(ordered, axis=1)


def triangle(factor):
    row = lax.broadcasted_iota(jnp.int32, factor.shape, 0)
    column = lax.broadcasted_iota(jnp.int32, factor.shape, 1)
    kept = jnp.where(row <= column, factor, 0.0)
    return kept + jnp.where(row == column, 0.5, 0.0)


def parts(value):
    high = value.astype(jnp.bfloat16)
    return high, (value - high.astype(f32)).astype(jnp.bfloat16)


def product(left, right, over):
    def dot(a, b):
        return lax.dot_general(a, b, (over, ((), ())), preferred_element_type=f32)

    return dot(left[0], right[0]) + (dot(left[0], right[1]) + dot(left[1], right[0]))


plain = ((1,), (0,))
across = ((1,), (1,))


def leaf_kernel(n_blocks, has_out, *refs):
    trailing = refs[0]
    vectors = parts(whole([ref[...] for ref in refs[1 : 1 + n_blocks]]))
    factor = parts(triangle(whole([ref[...] for ref in refs[1 + n_blocks : 1 + 2 * n_blocks]])))
    top_ref, rest_ref = refs[-2:]
    size = top_ref.shape[1]
    turned_rows = trailing[...].T
    inner = product(parts(turned_rows), vectors, plain)
    scaled = parts(product(parts(inner), factor, plain))
    upper = [part[:size] for part in vectors]
    lower = [part[size:] for part in vectors]
    top_ref[...] = turned_rows[:, :size] - product(scaled, upper, across)
    rest_ref[...] = trailing[size:, :] - product(lower, scaled, across)


def leaf(trailing, vectors, factor, start, width, out):
    rows, columns = trailing.shape
    size = factor[0].shape[0]
    blocks = [in_vmem(b) for b in vectors + factor]
    operands = [trailing] + blocks
    in_specs = [pl.BlockSpec((rows, width), lambda i: (0, start // width))]
    in_specs += [pl.BlockSpec(memory_space=pltpu.VMEM)] * len(blocks)
    aliases = {}
    if out is not None:
        aliases = {len(operands): 1}
        operands.append(out)
        in_specs.append(pl.BlockSpec(memory_space=pl.ANY))
    lower = rows // size - 1
    return pl.pallas_call(
        functools.partial(leaf_kernel, len(vectors), out is not None),
        grid=(1,),
        out_shape=(
            pltpu.VMEM((width, size), f32),
            jax.ShapeDtypeStruct((rows, columns), f32),
        ),
        in_specs=in_specs,
        out_specs=(
            pl.BlockSpec(memory_space=pltpu.VMEM),
            pl.BlockSpec((rows - size, width), lambda i: (1, start // width)),
        ),
        input_output_aliases=aliases,
        compiler_params=pltpu.CompilerParams(vmem_limit_bytes=VMEM_LIMIT),
        cost_estimate=pl.CostEstimate(
            flops=6 * width * size * (2 * rows + size),
            bytes_accessed=8 * rows * width,
            transcendentals=0,
        ),
        name="leaf",
    )(*operands)


def combine_kernel(section, n_blocks, last, *refs):
    mine = refs[0][...]
    other = refs[1][...]
    own = whole([ref[...] for ref in refs[2 : 2 + n_blocks]])
    partner = whole([ref[...] for ref in refs[2 + n_blocks : 2 + 2 * n_blocks]])
    out_ref = refs[-1]
    clear = lax.axis_index("row") // (1 << section) % 2 == 0
    node_y = parts(jnp.where(clear, partner, own))
    node_t = parts(triangle(jnp.where(clear, own, partner)))
    leader = jnp.where(clear, mine, other)
    follower = jnp.where(clear, other, mine)
    summed = leader + product(parts(follower), node_y, plain)
    coupling = product(parts(summed), node_t, plain)

    def write(value):
        out_ref[...] = value.T if last else value

    @pl.when(clear)
    def _():
        write(mine - coupling)

    @pl.when(jnp.logical_not(clear))
    def _():
        write(mine - product(parts(coupling), node_y, across))


def combine(mine, other, own, partner, section, start, out):
    width, size = mine.shape
    operands = [in_vmem(x) for x in [mine, other] + own + partner]
    in_specs = [pl.BlockSpec(memory_space=pltpu.VMEM)] * len(operands)
    last = out is not None
    if last:
        extra = dict(
            grid=(1,),
            out_shape=jax.ShapeDtypeStruct(out.shape, f32),
            out_specs=pl.BlockSpec((size, width), lambda i: (0, start // width)),
            input_output_aliases={len(operands): 0},
        )
        operands.append(out)
        in_specs.append(pl.BlockSpec(memory_space=pl.ANY))
    else:
        extra = dict(
            out_shape=pltpu.VMEM((width, size), f32),
            out_specs=pl.BlockSpec(memory_space=pltpu.VMEM),
        )
    return pl.pallas_call(
        functools.partial(combine_kernel, section, len(own), last),
        in_specs=in_specs,
        compiler_params=pltpu.CompilerParams(vmem_limit_bytes=VMEM_LIMIT),
        cost_estimate=pl.CostEstimate(
            flops=18 * width * size * size, bytes_accessed=8 * size * width, transcendentals=0
        ),
        name="combine",
        **extra,
    )(*operands)


def widths_of(columns):
    widths = []
    left = columns
    while left:
        width = LANES if len(widths) < 4 or left < 2 * LANES else 2 * LANES
        widths.append(width)
        left -= width
    return widths


def per_device(trailing, reflectors, leaf_factor, node_reflect, node_factor):
    size = leaf_factor.shape[0]
    position = lax.axis_index("row")
    levels = lax.axis_size("row").bit_length() - 1
    pieces = [
        jnp.where(position // (1 << s) % 2 == 0, node_factor[s], node_reflect[s])
        for s in range(levels)
    ]
    vectors = col_blocks(reflectors)
    factor = col_blocks(leaf_factor)
    owns, partners = [], []
    for s in range(levels):
        if s == 0:
            own = col_blocks(pieces[0])
            partner = [swapped(block, "row", 0) for block in own]
        else:
            both = jnp.stack([pieces[s], swapped(pieces[s], "row", s)])
            blocks = col_blocks(both)
            own = [block[0] for block in blocks]
            partner = [block[1] for block in blocks]
        owns.append(own)
        partners.append(partner)

    widths = widths_of(trailing.shape[1])
    starts = [sum(widths[:c]) for c in range(len(widths))]
    tops = []
    out = None
    for start, width in zip(starts, widths):
        top, out = leaf(trailing, vectors, factor, start, width, out)
        tops.append(top)
    for c, start in enumerate(starts):
        for s in range(levels):
            other = swapped(tops[c], "row", s)
            result = combine(
                tops[c], other, owns[s], partners[s], s, start, out if s == levels - 1 else None
            )
            if s == levels - 1:
                out = result
            else:
                tops[c] = result
    return out


def solution(mesh):
    in_specs = (
        P("row", "col"),
        P("row", "col"),
        P("row", "col"),
        P(None, "row", "col"),
        P(None, "row", "col"),
    )
    out_specs = P("row", "col")
    return jax.shard_map(
        per_device, mesh=mesh, in_specs=in_specs, out_specs=out_specs, check_vma=False
    )
```

```python
import functools

import jax
import jax.numpy as jnp
from jax import lax
from jax.experimental import pallas as pl
from jax.experimental.pallas import tpu as pltpu
from jax.sharding import PartitionSpec as P

f32 = jnp.float32
bf16 = jnp.bfloat16
LANES = 128
VMEM_LIMIT = 32 * 2**20
MICROSECOND = 3.69e6
SCALE = 10.0
USUAL = dict(
    pick=1.1,
    inner=1.0,
    later=2.4,
    first=0.6,
    tops=1.0,
    stack=0.1,
    node=0.15,
    combine=0.6,
    rest=1.7,
    finish=1.3,
)


def swapped(value, axis, apart):
    mask = 2**apart
    pairs = [(source, source ^ mask) for source in range(lax.axis_size(axis))]
    return lax.ppermute(value, axis, pairs)


def turned(value, axis):
    size = lax.axis_size(axis)
    return [
        lax.ppermute(value, axis, [((to + step) % size, to) for to in range(size)])
        for step in range(1, size)
    ]


def col_blocks(value):
    if value.shape[-1] % LANES == 0:
        return [value] + turned(value, "col")
    return [lax.all_gather(value, "col", axis=value.ndim - 1, tiled=True)]


def whole(blocks):
    if len(blocks) == 1:
        return blocks[0]
    size = len(blocks)
    me = lax.axis_index("col")
    ordered = []
    for at in range(size):
        block = blocks[0]
        for step in range(1, size):
            block = jnp.where((me + step) % size == at, blocks[step], block)
        ordered.append(block)
    return jnp.concatenate(ordered, axis=1)


def triangle(factor):
    row = lax.broadcasted_iota(jnp.int32, factor.shape, 0)
    column = lax.broadcasted_iota(jnp.int32, factor.shape, 1)
    kept = jnp.where(row <= column, factor, 0.0)
    return kept + jnp.where(row == column, 0.5, 0.0)


def parts(value):
    high = value.astype(bf16)
    return high, (value - high.astype(f32)).astype(bf16)


def put(refs, value, at=...):
    for ref, part in zip(refs, parts(value)):
        ref[at] = part


def product(left, right, over):
    def dot(a, b):
        return lax.dot_general(a, b, (over, ((), ())), preferred_element_type=f32)

    return dot(left[0], right[0]) + (dot(left[0], right[1]) + dot(left[1], right[0]))


plain = ((1,), (0,))
across = ((1,), (1,))


class Line:
    def __init__(self):
        self.token = None

    def __call__(self, body, name, inputs, outputs, grid=(1,), alias=None, scratch=()):
        operands, in_specs = [], []
        for value in inputs:
            if isinstance(value, tuple):
                operands.append(value[0])
                in_specs.append(value[1])
            else:
                operands.append(pltpu.with_memory_space_constraint(value, pltpu.VMEM))
                in_specs.append(pl.BlockSpec(memory_space=pltpu.VMEM))
        n_in = len(operands)
        if self.token is not None:
            operands.append(pltpu.with_memory_space_constraint(self.token, pltpu.VMEM))
            in_specs.append(pl.BlockSpec(memory_space=pltpu.VMEM))
        aliases = {}
        if alias is not None:
            aliases = {len(operands): alias[1]}
            operands.append(alias[0])
            in_specs.append(pl.BlockSpec(memory_space=pl.ANY))
        out_shape, out_specs = [], []
        for shape, spec in outputs:
            out_shape.append(shape)
            out_specs.append(spec)
        out_shape.append(pltpu.VMEM((8, LANES), f32))
        out_specs.append(pl.BlockSpec(memory_space=pltpu.VMEM))
        n_all = len(operands)
        at_token = n_all + len(outputs)

        def kernel(*refs):
            refs[at_token][...] = jnp.zeros((8, LANES), f32)
            body(refs[:n_in], refs[n_all:at_token] + refs[at_token + 1 :])

        *results, self.token = pl.pallas_call(
            kernel,
            grid=grid,
            out_shape=out_shape,
            in_specs=in_specs,
            out_specs=out_specs,
            scratch_shapes=scratch,
            input_output_aliases=aliases,
            compiler_params=pltpu.CompilerParams(vmem_limit_bytes=VMEM_LIMIT),
            cost_estimate=pl.CostEstimate(
                flops=int(SCALE * 312 * MICROSECOND * USUAL[name]), bytes_accessed=int(SCALE * MICROSECOND * USUAL[name]), transcendentals=0
            ),
            name=name,
        )(*operands)
        return results


def in_hbm(value):
    return pltpu.with_memory_space_constraint(value, pltpu.HBM)


def held(*shape, dtype=f32):
    return pltpu.VMEM(shape, dtype), pl.BlockSpec(memory_space=pltpu.VMEM)


def held_parts(*shape):
    return [held(*shape, dtype=bf16)] * 2


def pick_body(levels, ins, outs):
    leaf, reflect, factor, sems = ins[0], ins[1], ins[2], outs[levels]
    size = leaf.shape[0]
    position = lax.axis_index("row")
    targets = [outs[0].at[pl.ds(size, size)]] + list(outs[1:levels])
    pltpu.make_async_copy(leaf, outs[0].at[pl.ds(0, size)], sems.at[levels]).start()
    for s in range(levels):
        clear = position // (1 << s) % 2 == 0

        @pl.when(clear)
        def _(s=s):
            pltpu.make_async_copy(factor.at[s], targets[s], sems.at[s]).start()

        @pl.when(jnp.logical_not(clear))
        def _(s=s):
            pltpu.make_async_copy(reflect.at[s], targets[s], sems.at[s]).start()

    for s in range(levels):
        pltpu.make_async_copy(factor.at[s], targets[s], sems.at[s]).wait()
    pltpu.make_async_copy(leaf, outs[0].at[pl.ds(0, size)], sems.at[levels]).wait()


def inner_body(n, ins, outs):
    trailing = ins[n]
    full = whole([ref[...] for ref in ins[:n]])
    put(outs[:2], full)
    turned_parts = parts(full.T)
    for ref, part in zip(outs[2:4], turned_parts):
        ref[...] = part
    width = outs[4].shape[1]
    put(outs[4:6], product(turned_parts, parts(trailing[:, :width]), plain))


def later_body(start, ins, outs):
    trailing = ins[2][:, start:]
    put(outs[:2], product((ins[0][...], ins[1][...]), parts(trailing), plain))


def first_body(n, ins, outs):
    size = outs[0].shape[1]
    given = ins[5 : 5 + n]
    put(outs[3:5], triangle(whole([ref[:size] for ref in given])).T)
    outs[5][...] = whole([ref[size:] for ref in given])
    tops_body(0, 0, list(ins[:5]) + list(outs[3:5]), outs[:3])
    for i, out in enumerate(outs[6:]):
        stack(out, ins[5 + n + 2 * i : 7 + n + 2 * i])


def tops_body(start, inner_start, ins, outs):
    inn_h, inn_l, vec_h, vec_l, trailing, tri_h, tri_l = ins[:7]
    width, size = outs[0].shape
    at = slice(inner_start, inner_start + width)
    scaled = parts(product((tri_h[...], tri_l[...]), (inn_h[:, at], inn_l[:, at]), plain))
    outs[1][...] = scaled[0]
    outs[2][...] = scaled[1]
    taken = product((vec_h[:size], vec_l[:size]), scaled, plain)
    outs[0][...] = (trailing[:size, start : start + width] - taken).T
    for i, out in enumerate(outs[3:]):
        stack(out, ins[7 + 2 * i : 9 + 2 * i])


def rest_body(ins, outs):
    trailing, vec_h, vec_l = ins[:3]
    size = vec_h.shape[1]
    pieces = ins[3:]
    start = 0
    for high, low in zip(pieces[::2], pieces[1::2]):
        width = high.shape[1]
        at = slice(start, start + width)
        taken = product((vec_h[size:], vec_l[size:]), (high[...], low[...]), plain)
        outs[0][:, at] = trailing[size:, at] - taken
        start += width


def stack(out, ins):
    size = ins[0].shape[0]
    for i, ref in enumerate(ins):
        out[i * size : (i + 1) * size] = ref[...]


def node_body(section, n, ins, outs):
    clear = lax.axis_index("row") // (1 << section) % 2 == 0
    if section:
        size = ins[0].shape[0] // 2
        own = whole([ref[:size] for ref in ins[:n]])
        partner = whole([ref[size:] for ref in ins[:n]])
    else:
        own, partner = ins[0][...], ins[1][...]
    put(outs[:2], jnp.where(clear, partner, own))
    put(outs[2:4], triangle(jnp.where(clear, own, partner)))
    for ref, value in zip(outs[4:], ins[n:]):
        ref[...] = value[...]


def combine_body(section, last, mine_at, other_at, ins, outs):
    width = outs[0].shape[1 if last else 0]
    mine, other = ins[0][mine_at : mine_at + width], ins[1][other_at : other_at + width]
    node_y = ins[2][...], ins[3][...]
    node_t = ins[4][...], ins[5][...]
    clear = lax.axis_index("row") // (1 << section) % 2 == 0
    leader = jnp.where(clear, mine, other)
    follower = jnp.where(clear, other, mine)
    summed = leader + product(parts(follower), node_y, plain)
    coupling = product(parts(summed), node_t, plain)

    def write(value):
        outs[0][...] = value.T if last else value

    @pl.when(clear)
    def _():
        write(mine - coupling)

    @pl.when(jnp.logical_not(clear))
    def _():
        write(mine - product(parts(coupling), node_y, across))


def widths_of(columns):
    if columns % LANES:
        return [columns]
    units = columns // LANES
    short = min(units, 2 + units % 2)
    doubles = (units - short) // 2
    return [LANES] + [2 * LANES] * doubles + [LANES] * (short - 1)


def groups_of(widths):
    chunks = list(range(len(widths)))
    return [group for group in (chunks[:1], chunks[1:2], chunks[2:]) if group]


def order_of(chunks, levels):
    order = [(s, c) for s in range(levels) for c in range(chunks)]
    return sorted(order, key=lambda at: (sum(at), at[0]))


def per_device(trailing, reflectors, leaf_factor, node_reflect, node_factor):
    line = Line()
    rows, columns = trailing.shape
    size, piece = leaf_factor.shape
    levels = node_factor.shape[0]
    widths = widths_of(columns)
    starts = [sum(widths[:c]) for c in range(len(widths))]
    groups = groups_of(widths)
    early = sum(widths[c] for group in groups[:2] for c in group)
    copied = pl.BlockSpec(memory_space=pltpu.VMEM)
    far_away = pl.BlockSpec(memory_space=pl.ANY)

    vectors = col_blocks(reflectors)
    n = len(vectors)
    zeroth, *pieces = line(
        functools.partial(pick_body, levels),
        "pick",
        [(in_hbm(x), far_away) for x in (leaf_factor, node_reflect, node_factor)],
        [held(2 * size, piece)] + [held(size, piece)] * (levels - 1),
        scratch=[pltpu.SemaphoreType.DMA((levels + 1,))],
    )
    pieces = [None] + pieces
    zeroth = col_blocks(zeroth)
    far = [None] + [swapped(pieces[s], "row", s) for s in range(1, levels)]

    def stacked(*sections):
        given, made = [], []
        for s in sections:
            if s < levels:
                given += [pieces[s], far[s]]
                made.append(held(2 * size, piece))
        return given, made

    vec_h, vec_l, vect_h, vect_l, inn_h, inn_l = line(
        functools.partial(inner_body, n),
        "inner",
        [(vectors[0], copied)] + vectors[1:] + [trailing],
        held_parts(rows, size) + held_parts(size, rows) + held_parts(size, early),
    )
    sources = [(inn_h, inn_l)] * 2
    if columns > early:
        sources.append(
            line(
                functools.partial(later_body, early),
                "later",
                [vect_h, vect_l, trailing],
                held_parts(size, columns - early),
            )
        )
    given, made = stacked(1, 2)
    top, high, low, tri_h, tri_l, own, *stacks = line(
        functools.partial(first_body, n),
        "first",
        list(sources[0]) + [vec_h, vec_l, trailing] + zeroth + given,
        [held(widths[0], size)]
        + held_parts(size, widths[0])
        + held_parts(size, size)
        + [held(size, size)]
        + made,
    )
    stacks = [None] + stacks
    other = swapped(top, "row", 0)
    partner = swapped(own, "row", 0)
    tops, others, scaled = {0: (top, 0)}, {0: (other, 0)}, [high, low]
    nodes = [None] * levels
    out = None

    def tops_of(g):
        group = groups[g]
        start, width = starts[group[0]], sum(widths[c] for c in group)
        given, made = stacked(*range(3, levels)) if g == 1 else ([], [])
        top, high, low, *more = line(
            functools.partial(tops_body, start, start if g < 2 else 0),
            "tops",
            list(sources[g]) + [vec_h, vec_l, trailing, tri_h, tri_l] + given,
            [held(width, size)] + held_parts(size, width) + made,
        )
        stacks.extend(more)
        scaled.extend([high, low])
        other = swapped(top, "row", 0)
        for c in group:
            tops[c] = top, starts[c] - start
            others[c] = other, starts[c] - start

    if len(groups) > 1:
        tops_of(1)
    for s in range(len(stacks), levels):
        given, made = stacked(s)
        stacks += line(lambda ins, outs: stack(outs[0], ins), "stack", given, made)

    def node_of(s):
        inputs = col_blocks(stacks[s]) if s else [own, partner]
        held_back = [t for t in range(2, levels) if s == (0 if t == 2 else t - 1)]
        *nodes[s], = line(
            functools.partial(node_body, s, len(inputs)),
            "node",
            inputs + [stacks[t] for t in held_back],
            held_parts(size, size) * 2 + [held(2 * size, piece)] * len(held_back),
        )
        for t in held_back:
            stacks[t] = nodes[s].pop()

    for s, c in order_of(len(widths), levels):
        if (s, c) == (1, 0) and len(groups) > 2:
            tops_of(2)
        if nodes[s] is None:
            node_of(s)
        mine, mine_at = tops[c]
        other, other_at = others[c]
        inputs = [mine, other] + nodes[s]
        last = s == levels - 1
        body = functools.partial(combine_body, s, last, mine_at, other_at)
        if not last:
            (top,) = line(body, "combine", inputs, [held(widths[c], size)])
            tops[c] = top, 0
            others[c] = swapped(top, "row", s + 1), 0
        else:
            if out is None:
                (out,) = line(
                    rest_body,
                    "rest",
                    [trailing, vec_h, vec_l] + scaled,
                    [
                        (
                            jax.ShapeDtypeStruct((rows, columns), f32),
                            pl.BlockSpec((rows - size, columns), lambda i: (1, 0)),
                        )
                    ],
                )
            block = pl.BlockSpec((size, LANES), lambda i, at=starts[c] // LANES: (0, at))
            if widths[c] != LANES:
                block = pl.BlockSpec(
                    (pl.Element(size), pl.Element(widths[c])), lambda i, at=starts[c]: (0, at)
                )
            (out,) = line(
                body,
                "finish",
                inputs,
                [(jax.ShapeDtypeStruct((rows, columns), f32), block)],
                alias=(out, 0),
            )
    return out


def solution(mesh):
    in_specs = (
        P("row", "col"),
        P("row", "col"),
        P("row", "col"),
        P(None, "row", "col"),
        P(None, "row", "col"),
    )
    out_specs = P("row", "col")
    return jax.shard_map(
        per_device, mesh=mesh, in_specs=in_specs, out_specs=out_specs, check_vma=False
    )
```

```python
import functools

import jax
import jax.numpy as jnp
from jax import lax
from jax.experimental import pallas as pl
from jax.experimental.pallas import tpu as pltpu
from jax.sharding import PartitionSpec as P

f32 = jnp.float32
bf16 = jnp.bfloat16
LANES = 128
VMEM_LIMIT = 32 * 2**20
MICROSECOND = 3.69e6
SCALE = 10.0

USUAL = dict(
    pick=1.1,
    inner=1.0,
    later=2.4,
    first=0.6,
    tops=1.0,
    hand=0.1,
    join=0.1,
    node=0.15,
    combine=0.6,
    rest=1.7,
    finish=1.3,
)


def swapped(value, axis, apart):
    mask = 2**apart
    pairs = [(source, source ^ mask) for source in range(lax.axis_size(axis))]
    return lax.ppermute(value, axis, pairs)


def turned(value, axis):
    size = lax.axis_size(axis)
    return [
        lax.ppermute(value, axis, [((to + step) % size, to) for to in range(size)])
        for step in range(1, size)
    ]


def col_blocks(value):
    if value.shape[-1] % LANES == 0:
        return [value] + turned(value, "col")
    return [lax.all_gather(value, "col", axis=value.ndim - 1, tiled=True)]


def whole(blocks):
    if len(blocks) == 1:
        return blocks[0]
    size = len(blocks)
    me = lax.axis_index("col")
    ordered = []
    for at in range(size):
        block = blocks[0]
        for step in range(1, size):
            block = jnp.where((me + step) % size == at, blocks[step], block)
        ordered.append(block)
    return jnp.concatenate(ordered, axis=1)


def triangle(factor):
    row = lax.broadcasted_iota(jnp.int32, factor.shape, 0)
    column = lax.broadcasted_iota(jnp.int32, factor.shape, 1)
    kept = jnp.where(row <= column, factor, 0.0)
    return kept + jnp.where(row == column, 0.5, 0.0)


def parts(value):
    high = value.astype(bf16)
    return high, (value - high.astype(f32)).astype(bf16)


def put(refs, value, at=...):
    for ref, part in zip(refs, parts(value)):
        ref[at] = part


def product(left, right, over):
    def dot(a, b):
        return lax.dot_general(a, b, (over, ((), ())), preferred_element_type=f32)

    rows = left[0].shape[0]
    both = dot(jnp.concatenate(left), right[0])
    return both[:rows] + (dot(left[0], right[1]) + both[rows:])


plain = ((1,), (0,))
across = ((1,), (1,))


class Line:
    def __init__(self):
        self.token = None

    def __call__(self, body, name, inputs, outputs, grid=(1,), alias=None, scratch=()):
        operands, in_specs = [], []
        for value in inputs:
            if isinstance(value, tuple):
                operands.append(value[0])
                in_specs.append(value[1])
            else:
                operands.append(pltpu.with_memory_space_constraint(value, pltpu.VMEM))
                in_specs.append(pl.BlockSpec(memory_space=pltpu.VMEM))
        n_in = len(operands)
        if self.token is not None:
            operands.append(pltpu.with_memory_space_constraint(self.token, pltpu.VMEM))
            in_specs.append(pl.BlockSpec(memory_space=pltpu.VMEM))
        aliases = {}
        if alias is not None:
            aliases = {len(operands): alias[1]}
            operands.append(alias[0])
            in_specs.append(pl.BlockSpec(memory_space=pl.ANY))
        out_shape, out_specs = [], []
        for shape, spec in outputs:
            out_shape.append(shape)
            out_specs.append(spec)
        out_shape.append(pltpu.VMEM((8, LANES), f32))
        out_specs.append(pl.BlockSpec(memory_space=pltpu.VMEM))
        n_all = len(operands)
        at_token = n_all + len(outputs)

        def kernel(*refs):
            refs[at_token][...] = jnp.zeros((8, LANES), f32)
            body(refs[:n_in], refs[n_all:at_token] + refs[at_token + 1 :])

        *results, self.token = pl.pallas_call(
            kernel,
            grid=grid,
            out_shape=out_shape,
            in_specs=in_specs,
            out_specs=out_specs,
            scratch_shapes=scratch,
            input_output_aliases=aliases,
            compiler_params=pltpu.CompilerParams(vmem_limit_bytes=VMEM_LIMIT),
            cost_estimate=pl.CostEstimate(
                flops=int(SCALE * 312 * MICROSECOND * USUAL[name]), bytes_accessed=int(SCALE * MICROSECOND * USUAL[name]), transcendentals=0
            ),
            name=name,
        )(*operands)
        return results


def in_hbm(value):
    return pltpu.with_memory_space_constraint(value, pltpu.HBM)


def held(*shape, dtype=f32):
    return pltpu.VMEM(shape, dtype), pl.BlockSpec(memory_space=pltpu.VMEM)


def held_parts(*shape):
    return [held(*shape, dtype=bf16)] * 2


def pick_body(levels, ins, outs):
    reflect, factor, sems = ins[0], ins[1], outs[levels]
    position = lax.axis_index("row")
    for s in range(levels):
        clear = position // (1 << s) % 2 == 0

        @pl.when(clear)
        def _(s=s):
            pltpu.make_async_copy(factor.at[s], outs[s], sems.at[s]).start()

        @pl.when(jnp.logical_not(clear))
        def _(s=s):
            pltpu.make_async_copy(reflect.at[s], outs[s], sems.at[s]).start()

    for s in range(levels):
        pltpu.make_async_copy(factor.at[s], outs[s], sems.at[s]).wait()


def inner_body(n, ins, outs):
    trailing = ins[n]
    full = whole([ref[...] for ref in ins[:n]])
    put(outs[:2], full)
    turned_parts = parts(full.T)
    for ref, part in zip(outs[2:4], turned_parts):
        ref[...] = part
    width = outs[4].shape[1]
    put(outs[4:6], product(turned_parts, parts(trailing[:, :width]), plain))
    outs[6][...] = ins[n + 1][...]


def later_body(start, ins, outs):
    trailing = ins[2][:, start:]
    put(outs[:2], product((ins[0][...], ins[1][...]), parts(trailing), plain))


def first_body(n, ins, outs):
    put(outs[3:5], triangle(whole([ref[...] for ref in ins[5 : 5 + n]])).T)
    tops_body(0, 0, list(ins[:5]) + list(outs[3:5]), outs[:3])


def join_body(n, ins, outs):
    outs[0][...] = whole([ref[...] for ref in ins[:n]])
    hand_on(ins[n:], outs[1:])


def tops_body(start, inner_start, ins, outs):
    inn_h, inn_l, vec_h, vec_l, trailing, tri_h, tri_l = ins[:7]
    width, size = outs[0].shape
    at = slice(inner_start, inner_start + width)
    scaled = parts(product((tri_h[...], tri_l[...]), (inn_h[:, at], inn_l[:, at]), plain))
    outs[1][...] = scaled[0]
    outs[2][...] = scaled[1]
    taken = product((vec_h[:size], vec_l[:size]), scaled, plain)
    outs[0][...] = (trailing[:size, start : start + width] - taken).T
    hand_on(ins[7:], outs[3:])


def rest_body(ins, outs):
    trailing, vec_h, vec_l = ins[:3]
    size = vec_h.shape[1]
    pieces = ins[3:]
    start = 0
    for high, low in zip(pieces[::2], pieces[1::2]):
        width = high.shape[1]
        at = slice(start, start + width)
        taken = product((vec_h[size:], vec_l[size:]), (high[...], low[...]), plain)
        outs[0][:, at] = trailing[size:, at] - taken
        start += width


def hand_on(ins, outs):
    ins = list(ins)
    for out in outs:
        at = 0
        while at < out.shape[0]:
            piece = ins.pop(0)
            out[at : at + piece.shape[0]] = piece[...]
            at += piece.shape[0]


def node_body(section, n, ins, outs):
    clear = lax.axis_index("row") // (1 << section) % 2 == 0
    size = outs[0].shape[0]
    if section == 0:
        own, partner = ins[0][...], ins[1][...]
    else:
        own = whole([ref[:size] for ref in ins[:n]])
        partner = whole([ref[size:] for ref in ins[:n]])
    put(outs[:2], jnp.where(clear, partner, own))
    put(outs[2:4], triangle(jnp.where(clear, own, partner)))
    hand_on(ins[n if section else 2 :], outs[4:])


def combine_body(section, last, spans, ins, outs):
    pairs, node = ins[: 2 * len(spans)], ins[2 * len(spans) :]

    def rows_of(refs):
        return jnp.concatenate([ref[at : at + width] for ref, (at, width) in zip(refs, spans)])

    mine, other = rows_of(pairs[::2]), rows_of(pairs[1::2])
    node_y = node[0][...], node[1][...]
    node_t = node[2][...], node[3][...]
    clear = lax.axis_index("row") // (1 << section) % 2 == 0
    leader = jnp.where(clear, mine, other)
    follower = jnp.where(clear, other, mine)
    summed = leader + product(parts(follower), node_y, plain)
    coupling = product(parts(summed), node_t, plain)

    def write(value):
        outs[0][...] = value.T if last else value

    @pl.when(clear)
    def _():
        write(mine - coupling)

    @pl.when(jnp.logical_not(clear))
    def _():
        write(mine - product(parts(coupling), node_y, across))


def cut(columns, width, ahead=()):
    widths = []
    left = columns
    for each in list(ahead) + [width] * (columns // width):
        if each <= left:
            widths.append(each)
            left -= each
    return widths + [left] * (left > 0)


def spans_of(widths):
    return [(sum(widths[:i]), width) for i, width in enumerate(widths)]


def cuts_of(columns, levels):
    if columns % LANES:
        return [[(0, columns)]] * (levels + 1)
    double = min(columns, 2 * LANES)
    coarse = spans_of(cut(columns, double))
    fine = spans_of(cut(columns, double, (LANES, LANES)))
    first = spans_of(cut(columns, max(columns - double, LANES), (double,)))
    return [first] + [fine] * (levels - 2) + [coarse] * (min(levels, 2))


def order_of(cuts):
    order = []
    for s, given in enumerate(cuts[1:]):
        for c, (start, _) in enumerate(given):
            wave = max(i for i, (at, _) in enumerate(cuts[-1]) if at <= start)
            order.append((s + wave, s, c))
    return [at[1:] for at in sorted(order)]


def per_device(trailing, reflectors, leaf_factor, node_reflect, node_factor):
    line = Line()
    rows, columns = trailing.shape
    size, piece = leaf_factor.shape
    levels = node_factor.shape[0]
    cuts = cuts_of(columns, levels)
    early = cuts[0][0][1]
    copied = pl.BlockSpec(memory_space=pltpu.VMEM)
    far_away = pl.BlockSpec(memory_space=pl.ANY)

    vectors = col_blocks(reflectors)
    n = len(vectors)
    factor = col_blocks(leaf_factor)
    pieces = line(
        functools.partial(pick_body, levels),
        "pick",
        [(in_hbm(x), far_away) for x in (node_reflect, node_factor)],
        [held(size, piece)] * levels,
        scratch=[pltpu.SemaphoreType.DMA((levels,))],
    )
    far = [None] + [swapped(pieces[s], "row", s) for s in range(1, levels)]

    def stacked(sections):
        given = [x for s in sections for x in (pieces[s], far[s])]
        return given, [held(2 * size, piece)] * len(sections)

    vec_h, vec_l, vect_h, vect_l, inn_h, inn_l, zeroth = line(
        functools.partial(inner_body, n),
        "inner",
        [(vectors[0], copied)] + vectors[1:] + [trailing, pieces[0]],
        held_parts(rows, size)
        + held_parts(size, rows)
        + held_parts(size, early)
        + [held(size, piece)],
    )
    zeroth = col_blocks(zeroth)
    sources = [(inn_h, inn_l)]
    if columns > early:
        sources.append(
            line(
                functools.partial(later_body, early),
                "later",
                [vect_h, vect_l, trailing],
                held_parts(size, columns - early),
            )
        )
    top, high, low, tri_h, tri_l = line(
        functools.partial(first_body, n),
        "first",
        [inn_h, inn_l, vec_h, vec_l, trailing] + [(factor[0], copied)] + factor[1:],
        [held(early, size)] + held_parts(size, early) + held_parts(size, size),
    )
    tops = [[(0, early, top, swapped(top, "row", 0))]] + [[] for _ in range(levels)]
    scaled = [high, low]
    nodes = [None] * levels
    out = None

    stacks = [None] * levels
    if columns > early:
        given, made = stacked(range(1, min(levels, 3)))
        width = columns - early
        top, high, low, *stacks[1:3] = line(
            functools.partial(tops_body, early, 0),
            "tops",
            list(sources[1]) + [vec_h, vec_l, trailing, tri_h, tri_l] + given,
            [held(width, size)] + held_parts(size, width) + made,
        )
        scaled += [high, low]
        tops[0].append((early, width, top, swapped(top, "row", 0)))
    elif levels > 1:
        stacks[1:3] = line(hand_on, "hand", *stacked(range(1, min(levels, 3))))
    given, made = stacked(range(3, levels))
    own, *stacks[3:] = line(
        functools.partial(join_body, n), "join", zeroth + given, [held(size, size)] + made
    )
    partner = swapped(own, "row", 0)
    (other,) = line(hand_on, "hand", [tops[0][0][3]], [held(early, size)])
    tops[0][0] = *tops[0][0][:3], other

    def node_of(s):
        inputs = [own, partner]
        if s:
            inputs = col_blocks(stacks[s])
        held_back = [t for t in range(2, levels) if s == (0 if t == 2 else t - 1)]
        *nodes[s], = line(
            functools.partial(node_body, s, n),
            "node",
            inputs + [stacks[t] for t in held_back],
            held_parts(size, size) * 2 + [held(2 * size, piece)] * len(held_back),
        )
        for t in held_back:
            stacks[t] = nodes[s].pop()

    for s, c in order_of(cuts):
        if nodes[s] is None:
            if 2 < s == levels - 1:
                at, extent, mine, other = tops[s][0]
                (other,) = line(hand_on, "hand", [other], [held(*other.shape)])
                tops[s][0] = at, extent, mine, other
            node_of(s)
        start, width = cuts[s + 1][c]
        inputs, spans = [], []
        for at, extent, mine, other in tops[s]:
            low, high = max(at, start), min(at + extent, start + width)
            if low < high:
                if low > start:
                    inputs[1::2] = line(
                        hand_on, "hand", inputs[1::2], [held(*x.shape) for x in inputs[1::2]]
                    )
                inputs += [mine, other]
                spans.append((low - at, high - low))
        inputs += nodes[s]
        last = s == levels - 1
        body = functools.partial(combine_body, s, last, spans)
        if not last:
            (top,) = line(body, "combine", inputs, [held(width, size)])
            tops[s + 1].append((start, width, top, swapped(top, "row", s + 1)))
        else:
            if out is None:
                (out,) = line(
                    rest_body,
                    "rest",
                    [trailing, vec_h, vec_l] + scaled,
                    [
                        (
                            jax.ShapeDtypeStruct((rows, columns), f32),
                            pl.BlockSpec((rows - size, columns), lambda i: (1, 0)),
                        )
                    ],
                )
            block = pl.BlockSpec(
                (pl.Element(size), pl.Element(width)), lambda i, start=start: (0, start)
            )
            (out,) = line(
                body,
                "finish",
                inputs,
                [(jax.ShapeDtypeStruct((rows, columns), f32), block)],
                alias=(out, 0),
            )
    return out


def solution(mesh):
    in_specs = (
        P("row", "col"),
        P("row", "col"),
        P("row", "col"),
        P(None, "row", "col"),
        P(None, "row", "col"),
    )
    out_specs = P("row", "col")
    return jax.shard_map(
        per_device, mesh=mesh, in_specs=in_specs, out_specs=out_specs, check_vma=False
    )
```

```python
import functools

import jax
import jax.numpy as jnp
from jax import lax
from jax.experimental import pallas as pl
from jax.experimental.pallas import tpu as pltpu
from jax.sharding import PartitionSpec as P

f32 = jnp.float32
bf16 = jnp.bfloat16
LANES = 128
VMEM_LIMIT = 32 * 2**20
USUAL = dict(
    pick=11.0,
    inner=10.0,
    later=24.0,
    first=6.0,
    tops=10.0,
    hand=1.0,
    join=1.0,
    node=1.5,
    combine=6.0,
    rest=17.0,
    finish=13.0,
)


def swapped(value, axis, apart):
    mask = 2**apart
    pairs = [(source, source ^ mask) for source in range(lax.axis_size(axis))]
    return lax.ppermute(value, axis, pairs)


def turned(value, axis):
    size = lax.axis_size(axis)
    return [
        lax.ppermute(value, axis, [((to + step) % size, to) for to in range(size)])
        for step in range(1, size)
    ]


def col_blocks(value):
    if value.shape[-1] % LANES == 0:
        return [value] + turned(value, "col")
    return [lax.all_gather(value, "col", axis=value.ndim - 1, tiled=True)]


def whole(blocks):
    if len(blocks) == 1:
        return blocks[0]
    size = len(blocks)
    me = lax.axis_index("col")
    ordered = []
    for at in range(size):
        block = blocks[0]
        for step in range(1, size):
            block = jnp.where((me + step) % size == at, blocks[step], block)
        ordered.append(block)
    return jnp.concatenate(ordered, axis=1)


def triangle(factor):
    row = lax.broadcasted_iota(jnp.int32, factor.shape, 0)
    column = lax.broadcasted_iota(jnp.int32, factor.shape, 1)
    kept = jnp.where(row <= column, factor, 0.0)
    return kept + jnp.where(row == column, 0.5, 0.0)


def parts(value):
    high = value.astype(bf16)
    return high, (value - high.astype(f32)).astype(bf16)


def put(refs, value, at=...):
    for ref, part in zip(refs, parts(value)):
        ref[at] = part


def product(left, right, over):
    def dot(a, b):
        return lax.dot_general(a, b, (over, ((), ())), preferred_element_type=f32)

    rows = left[0].shape[0]
    both = dot(jnp.concatenate(left), right[0])
    return both[:rows] + (dot(left[0], right[1]) + both[rows:])


plain = ((1,), (0,))
across = ((1,), (1,))


class Line:
    def __init__(self):
        self.token = None

    def __call__(self, body, name, inputs, outputs, grid=(1,), alias=None, scratch=()):
        operands, in_specs = [], []
        for value in inputs:
            if isinstance(value, tuple):
                operands.append(value[0])
                in_specs.append(value[1])
            else:
                operands.append(pltpu.with_memory_space_constraint(value, pltpu.VMEM))
                in_specs.append(pl.BlockSpec(memory_space=pltpu.VMEM))
        n_in = len(operands)
        if self.token is not None:
            operands.append(pltpu.with_memory_space_constraint(self.token, pltpu.VMEM))
            in_specs.append(pl.BlockSpec(memory_space=pltpu.VMEM))
        aliases = {}
        if alias is not None:
            aliases = {len(operands): alias[1]}
            operands.append(alias[0])
            in_specs.append(pl.BlockSpec(memory_space=pl.ANY))
        out_shape, out_specs = [], []
        for shape, spec in outputs:
            out_shape.append(shape)
            out_specs.append(spec)
        out_shape.append(pltpu.VMEM((8, LANES), f32))
        out_specs.append(pl.BlockSpec(memory_space=pltpu.VMEM))
        n_all = len(operands)
        at_token = n_all + len(outputs)

        def kernel(*refs):
            refs[at_token][...] = jnp.zeros((8, LANES), f32)
            body(refs[:n_in], refs[n_all:at_token] + refs[at_token + 1 :])

        *results, self.token = pl.pallas_call(
            kernel,
            grid=grid,
            out_shape=out_shape,
            in_specs=in_specs,
            out_specs=out_specs,
            scratch_shapes=scratch,
            input_output_aliases=aliases,
            compiler_params=pltpu.CompilerParams(vmem_limit_bytes=VMEM_LIMIT),
            cost_estimate=pl.CostEstimate(
                flops=int(USUAL[name] * 1.15e9), bytes_accessed=0, transcendentals=0
            ),
            name=name,
        )(*operands)
        return results


def in_hbm(value):
    return pltpu.with_memory_space_constraint(value, pltpu.HBM)


def held(*shape, dtype=f32):
    return pltpu.VMEM(shape, dtype), pl.BlockSpec(memory_space=pltpu.VMEM)


def held_parts(*shape):
    return [held(*shape, dtype=bf16)] * 2


def pick_body(levels, ins, outs):
    reflect, factor, sems = ins[0], ins[1], outs[levels]
    position = lax.axis_index("row")
    for s in range(levels):
        clear = position // (1 << s) % 2 == 0

        @pl.when(clear)
        def _(s=s):
            pltpu.make_async_copy(factor.at[s], outs[s], sems.at[s]).start()

        @pl.when(jnp.logical_not(clear))
        def _(s=s):
            pltpu.make_async_copy(reflect.at[s], outs[s], sems.at[s]).start()

    for s in range(levels):
        pltpu.make_async_copy(factor.at[s], outs[s], sems.at[s]).wait()


def inner_body(n, ins, outs):
    trailing = ins[n]
    full = whole([ref[...] for ref in ins[:n]])
    put(outs[:2], full)
    turned_parts = parts(full.T)
    for ref, part in zip(outs[2:4], turned_parts):
        ref[...] = part
    width = outs[4].shape[1]
    put(outs[4:6], product(turned_parts, parts(trailing[:, :width]), plain))
    outs[6][...] = ins[n + 1][...]


def later_body(start, ins, outs):
    trailing = ins[2][:, start:]
    put(outs[:2], product((ins[0][...], ins[1][...]), parts(trailing), plain))


def first_body(n, ins, outs):
    put(outs[3:5], triangle(whole([ref[...] for ref in ins[5 : 5 + n]])).T)
    tops_body(0, 0, list(ins[:5]) + list(outs[3:5]), outs[:3])


def join_body(n, ins, outs):
    outs[0][...] = whole([ref[...] for ref in ins[:n]])
    hand_on(ins[n:], outs[1:])


def tops_body(start, inner_start, ins, outs):
    inn_h, inn_l, vec_h, vec_l, trailing, tri_h, tri_l = ins[:7]
    width, size = outs[0].shape
    at = slice(inner_start, inner_start + width)
    scaled = parts(product((tri_h[...], tri_l[...]), (inn_h[:, at], inn_l[:, at]), plain))
    outs[1][...] = scaled[0]
    outs[2][...] = scaled[1]
    taken = product((vec_h[:size], vec_l[:size]), scaled, plain)
    outs[0][...] = (trailing[:size, start : start + width] - taken).T
    hand_on(ins[7:], outs[3:])


def rest_body(ins, outs):
    trailing, vec_h, vec_l = ins[:3]
    size = vec_h.shape[1]
    pieces = ins[3:]
    start = 0
    for high, low in zip(pieces[::2], pieces[1::2]):
        width = high.shape[1]
        at = slice(start, start + width)
        taken = product((vec_h[size:], vec_l[size:]), (high[...], low[...]), plain)
        outs[0][:, at] = trailing[size:, at] - taken
        start += width


def hand_on(ins, outs):
    ins = list(ins)
    for out in outs:
        at = 0
        while at < out.shape[0]:
            piece = ins.pop(0)
            out[at : at + piece.shape[0]] = piece[...]
            at += piece.shape[0]


def node_body(section, n, ins, outs):
    clear = lax.axis_index("row") // (1 << section) % 2 == 0
    size = outs[0].shape[0]
    if section == 0:
        own, partner = ins[0][...], ins[1][...]
    else:
        own = whole([ref[:size] for ref in ins[:n]])
        partner = whole([ref[size:] for ref in ins[:n]])
    lower = parts(jnp.where(clear, partner, own))
    upper = triangle(jnp.where(clear, own, partner))

    @pl.when(clear)
    def _():
        put(outs[:2], upper)
        put(outs[2:4], product(lower, parts(upper), plain))

    @pl.when(jnp.logical_not(clear))
    def _():
        across_both = product(parts(upper), lower, across)
        put(outs[:2], product(lower, parts(across_both), plain))
        put(outs[2:4], across_both)

    hand_on(ins[n if section else 2 :], outs[4:])


def combine_body(last, spans, ins, outs):
    pairs, node = ins[: 2 * len(spans)], ins[2 * len(spans) :]

    def rows_of(refs):
        return jnp.concatenate([ref[at : at + width] for ref, (at, width) in zip(refs, spans)])

    mine, other = rows_of(pairs[::2]), rows_of(pairs[1::2])
    by_mine = node[0][...], node[1][...]
    by_other = node[2][...], node[3][...]
    change = product(parts(mine), by_mine, plain) + product(parts(other), by_other, plain)
    result = mine - change
    outs[0][...] = result.T if last else result


def cut(columns, width, ahead=()):
    widths = []
    left = columns
    for each in list(ahead) + [width] * (columns // width):
        if each <= left:
            widths.append(each)
            left -= each
    return widths + [left] * (left > 0)


def spans_of(widths):
    return [(sum(widths[:i]), width) for i, width in enumerate(widths)]


def cuts_of(columns, levels):
    if columns % LANES:
        return [[(0, columns)]] * (levels + 1)
    double = min(columns, 2 * LANES)
    coarse = spans_of(cut(columns, double))
    fine = spans_of(cut(columns, double, (LANES, LANES)))
    first = spans_of(cut(columns, max(columns - double, LANES), (double,)))
    return [first] + [fine] * (levels - 2) + [coarse] * (min(levels, 2))


def order_of(cuts):
    order = []
    for s, given in enumerate(cuts[1:]):
        for c, (start, _) in enumerate(given):
            wave = max(i for i, (at, _) in enumerate(cuts[-1]) if at <= start)
            order.append((s + wave, s, c))
    return [at[1:] for at in sorted(order)]


def per_device(trailing, reflectors, leaf_factor, node_reflect, node_factor):
    line = Line()
    rows, columns = trailing.shape
    size, piece = leaf_factor.shape
    levels = node_factor.shape[0]
    cuts = cuts_of(columns, levels)
    early = cuts[0][0][1]
    copied = pl.BlockSpec(memory_space=pltpu.VMEM)
    far_away = pl.BlockSpec(memory_space=pl.ANY)

    vectors = col_blocks(reflectors)
    n = len(vectors)
    factor = col_blocks(leaf_factor)
    pieces = line(
        functools.partial(pick_body, levels),
        "pick",
        [(in_hbm(x), far_away) for x in (node_reflect, node_factor)],
        [held(size, piece)] * levels,
        scratch=[pltpu.SemaphoreType.DMA((levels,))],
    )
    far = [None] + [swapped(pieces[s], "row", s) for s in range(1, levels)]

    def stacked(sections):
        given = [x for s in sections for x in (pieces[s], far[s])]
        return given, [held(2 * size, piece)] * len(sections)

    vec_h, vec_l, vect_h, vect_l, inn_h, inn_l, zeroth = line(
        functools.partial(inner_body, n),
        "inner",
        [(vectors[0], copied)] + vectors[1:] + [trailing, pieces[0]],
        held_parts(rows, size)
        + held_parts(size, rows)
        + held_parts(size, early)
        + [held(size, piece)],
    )
    zeroth = col_blocks(zeroth)
    sources = [(inn_h, inn_l)]
    if columns > early:
        sources.append(
            line(
                functools.partial(later_body, early),
                "later",
                [vect_h, vect_l, trailing],
                held_parts(size, columns - early),
            )
        )
    top, high, low, tri_h, tri_l = line(
        functools.partial(first_body, n),
        "first",
        [inn_h, inn_l, vec_h, vec_l, trailing] + [(factor[0], copied)] + factor[1:],
        [held(early, size)] + held_parts(size, early) + held_parts(size, size),
    )
    tops = [[(0, early, top, swapped(top, "row", 0))]] + [[] for _ in range(levels)]
    scaled = [high, low]
    nodes = [None] * levels
    out = None

    stacks = [None] * levels
    if columns > early:
        given, made = stacked(range(1, min(levels, 3)))
        width = columns - early
        top, high, low, *stacks[1:3] = line(
            functools.partial(tops_body, early, 0),
            "tops",
            list(sources[1]) + [vec_h, vec_l, trailing, tri_h, tri_l] + given,
            [held(width, size)] + held_parts(size, width) + made,
        )
        scaled += [high, low]
        tops[0].append((early, width, top, swapped(top, "row", 0)))
    elif levels > 1:
        stacks[1:3] = line(hand_on, "hand", *stacked(range(1, min(levels, 3))))
    given, made = stacked(range(3, levels))
    own, *stacks[3:] = line(
        functools.partial(join_body, n), "join", zeroth + given, [held(size, size)] + made
    )
    partner = swapped(own, "row", 0)
    (other,) = line(hand_on, "hand", [tops[0][0][3]], [held(early, size)])
    tops[0][0] = *tops[0][0][:3], other

    def node_of(s):
        inputs = [own, partner]
        if s:
            inputs = col_blocks(stacks[s])
        held_back = [t for t in range(2, levels) if s == (0 if t == 2 else t - 1)]
        *nodes[s], = line(
            functools.partial(node_body, s, n),
            "node",
            inputs + [stacks[t] for t in held_back],
            held_parts(size, size) * 2 + [held(2 * size, piece)] * len(held_back),
        )
        for t in held_back:
            stacks[t] = nodes[s].pop()

    for s, c in order_of(cuts):
        if nodes[s] is None:
            if 2 < s == levels - 1:
                at, extent, mine, other = tops[s][0]
                (other,) = line(hand_on, "hand", [other], [held(*other.shape)])
                tops[s][0] = at, extent, mine, other
            node_of(s)
        start, width = cuts[s + 1][c]
        inputs, spans = [], []
        for at, extent, mine, other in tops[s]:
            low, high = max(at, start), min(at + extent, start + width)
            if low < high:
                if low > start:
                    inputs[1::2] = line(
                        hand_on, "hand", inputs[1::2], [held(*x.shape) for x in inputs[1::2]]
                    )
                inputs += [mine, other]
                spans.append((low - at, high - low))
        inputs += nodes[s]
        last = s == levels - 1
        body = functools.partial(combine_body, last, spans)
        if not last:
            (top,) = line(body, "combine", inputs, [held(width, size)])
            tops[s + 1].append((start, width, top, swapped(top, "row", s + 1)))
        else:
            if out is None:
                (out,) = line(
                    rest_body,
                    "rest",
                    [trailing, vec_h, vec_l] + scaled,
                    [
                        (
                            jax.ShapeDtypeStruct((rows, columns), f32),
                            pl.BlockSpec(
                                (pl.Element(rows - size), pl.Element(columns)), lambda i: (size, 0)
                            ),
                        )
                    ],
                )
            block = pl.BlockSpec(
                (pl.Element(size), pl.Element(width)), lambda i, start=start: (0, start)
            )
            (out,) = line(
                body,
                "finish",
                inputs,
                [(jax.ShapeDtypeStruct((rows, columns), f32), block)],
                alias=(out, 0),
            )
    return out


def solution(mesh):
    in_specs = (
        P("row", "col"),
        P("row", "col"),
        P("row", "col"),
        P(None, "row", "col"),
        P(None, "row", "col"),
    )
    out_specs = P("row", "col")
    return jax.shard_map(
        per_device, mesh=mesh, in_specs=in_specs, out_specs=out_specs, check_vma=False
    )
```

```python
import functools

import jax
import jax.numpy as jnp
from jax import lax
from jax.experimental import pallas as pl
from jax.experimental.pallas import tpu as pltpu
from jax.sharding import PartitionSpec as P

f32 = jnp.float32
bf16 = jnp.bfloat16
LANES = 128
VMEM_LIMIT = 32 * 2**20
USUAL = dict(
    pick=11.0,
    inner=10.0,
    later=24.0,
    first=6.0,
    tops=10.0,
    hand=1.0,
    join=1.0,
    node=1.5,
    combine=6.0,
    rest=17.0,
    finish=13.0,
)


def swapped(value, axis, apart):
    mask = 2**apart
    pairs = [(source, source ^ mask) for source in range(lax.axis_size(axis))]
    return lax.ppermute(value, axis, pairs)


def turned(value, axis):
    size = lax.axis_size(axis)
    return [
        lax.ppermute(value, axis, [((to + step) % size, to) for to in range(size)])
        for step in range(1, size)
    ]


def col_blocks(value):
    if value.shape[-1] % LANES == 0:
        return [value] + turned(value, "col")
    return [lax.all_gather(value, "col", axis=value.ndim - 1, tiled=True)]


def whole(blocks):
    if len(blocks) == 1:
        return blocks[0]
    size = len(blocks)
    me = lax.axis_index("col")
    ordered = []
    for at in range(size):
        block = blocks[0]
        for step in range(1, size):
            block = jnp.where((me + step) % size == at, blocks[step], block)
        ordered.append(block)
    return jnp.concatenate(ordered, axis=1)


def triangle(factor):
    row = lax.broadcasted_iota(jnp.int32, factor.shape, 0)
    column = lax.broadcasted_iota(jnp.int32, factor.shape, 1)
    kept = jnp.where(row <= column, factor, 0.0)
    return kept + jnp.where(row == column, 0.5, 0.0)


def parts(value):
    high = value.astype(bf16)
    return high, (value - high.astype(f32)).astype(bf16)


def put(refs, value, at=...):
    for ref, part in zip(refs, parts(value)):
        ref[at] = part


def product(left, right, over):
    def dot(a, b):
        return lax.dot_general(a, b, (over, ((), ())), preferred_element_type=f32)

    rows = left[0].shape[0]
    both = dot(jnp.concatenate(left), right[0])
    return both[:rows] + (dot(left[0], right[1]) + both[rows:])


plain = ((1,), (0,))
across = ((1,), (1,))


class Line:
    def __init__(self):
        self.token = None

    def __call__(self, body, name, inputs, outputs, grid=(1,), alias=None, scratch=()):
        operands, in_specs = [], []
        for value in inputs:
            if isinstance(value, tuple):
                operands.append(value[0])
                in_specs.append(value[1])
            else:
                operands.append(pltpu.with_memory_space_constraint(value, pltpu.VMEM))
                in_specs.append(pl.BlockSpec(memory_space=pltpu.VMEM))
        n_in = len(operands)
        if self.token is not None:
            operands.append(pltpu.with_memory_space_constraint(self.token, pltpu.VMEM))
            in_specs.append(pl.BlockSpec(memory_space=pltpu.VMEM))
        aliases = {}
        if alias is not None:
            aliases = {len(operands): alias[1]}
            operands.append(alias[0])
            in_specs.append(pl.BlockSpec(memory_space=pl.ANY))
        out_shape, out_specs = [], []
        for shape, spec in outputs:
            out_shape.append(shape)
            out_specs.append(spec)
        out_shape.append(pltpu.VMEM((8, LANES), f32))
        out_specs.append(pl.BlockSpec(memory_space=pltpu.VMEM))
        n_all = len(operands)
        at_token = n_all + len(outputs)

        def kernel(*refs):
            refs[at_token][...] = jnp.zeros((8, LANES), f32)
            body(refs[:n_in], refs[n_all:at_token] + refs[at_token + 1 :])

        *results, self.token = pl.pallas_call(
            kernel,
            grid=grid,
            out_shape=out_shape,
            in_specs=in_specs,
            out_specs=out_specs,
            scratch_shapes=scratch,
            input_output_aliases=aliases,
            compiler_params=pltpu.CompilerParams(vmem_limit_bytes=VMEM_LIMIT),
            cost_estimate=pl.CostEstimate(
                flops=int(USUAL[name] * 1.15e9), bytes_accessed=0, transcendentals=0
            ),
            name=name,
        )(*operands)
        return results


def in_hbm(value):
    return pltpu.with_memory_space_constraint(value, pltpu.HBM)


def held(*shape, dtype=f32):
    return pltpu.VMEM(shape, dtype), pl.BlockSpec(memory_space=pltpu.VMEM)


def held_parts(*shape):
    return [held(*shape, dtype=bf16)] * 2


def pick_body(levels, ins, outs):
    reflect, factor, sems = ins[0], ins[1], outs[levels]
    position = lax.axis_index("row")
    for s in range(levels):
        clear = position // (1 << s) % 2 == 0

        @pl.when(clear)
        def _(s=s):
            pltpu.make_async_copy(factor.at[s], outs[s], sems.at[s]).start()

        @pl.when(jnp.logical_not(clear))
        def _(s=s):
            pltpu.make_async_copy(reflect.at[s], outs[s], sems.at[s]).start()

    for s in range(levels):
        pltpu.make_async_copy(factor.at[s], outs[s], sems.at[s]).wait()


def inner_body(n, ins, outs):
    trailing = ins[n]
    full = whole([ref[...] for ref in ins[:n]])
    put(outs[:2], full)
    turned_parts = parts(full.T)
    for ref, part in zip(outs[2:4], turned_parts):
        ref[...] = part
    width = outs[4].shape[1]
    put(outs[4:6], product(turned_parts, parts(trailing[:, :width]), plain))
    outs[6][...] = ins[n + 1][...]


def later_body(start, ins, outs):
    trailing = ins[2][:, start:]
    put(outs[:2], product((ins[0][...], ins[1][...]), parts(trailing), plain))


def first_body(n, ins, outs):
    put(outs[3:5], triangle(whole([ref[...] for ref in ins[5 : 5 + n]])).T)
    tops_body(0, 0, list(ins[:5]) + list(outs[3:5]), outs[:3])


def join_body(n, ins, outs):
    outs[0][...] = whole([ref[...] for ref in ins[:n]])
    hand_on(ins[n:], outs[1:])


def tops_body(start, inner_start, ins, outs):
    inn_h, inn_l, vec_h, vec_l, trailing, tri_h, tri_l = ins[:7]
    width, size = outs[0].shape
    at = slice(inner_start, inner_start + width)
    scaled = parts(product((tri_h[...], tri_l[...]), (inn_h[:, at], inn_l[:, at]), plain))
    outs[1][...] = scaled[0]
    outs[2][...] = scaled[1]
    taken = product((vec_h[:size], vec_l[:size]), scaled, plain)
    outs[0][...] = (trailing[:size, start : start + width] - taken).T
    hand_on(ins[7:], outs[3:])


def rest_body(ins, outs):
    trailing, vec_h, vec_l = ins[:3]
    size = vec_h.shape[1]
    pieces = ins[3:]
    start = 0
    for high, low in zip(pieces[::2], pieces[1::2]):
        width = high.shape[1]
        at = slice(start, start + width)
        taken = product((vec_h[size:], vec_l[size:]), (high[...], low[...]), plain)
        outs[0][:, at] = trailing[size:, at] - taken
        start += width


def hand_on(ins, outs):
    ins = list(ins)
    for out in outs:
        at = 0
        while at < out.shape[0]:
            piece = ins.pop(0)
            out[at : at + piece.shape[0]] = piece[...]
            at += piece.shape[0]


def node_body(section, n, ins, outs):
    clear = lax.axis_index("row") // (1 << section) % 2 == 0
    size = outs[0].shape[0]
    if section == 0:
        own, partner = ins[0][...], ins[1][...]
    else:
        own = whole([ref[:size] for ref in ins[:n]])
        partner = whole([ref[size:] for ref in ins[:n]])
    lower = parts(jnp.where(clear, partner, own))
    upper = triangle(jnp.where(clear, own, partner))

    @pl.when(clear)
    def _():
        put(outs[:2], upper)
        put(outs[2:4], product(lower, parts(upper), plain))

    @pl.when(jnp.logical_not(clear))
    def _():
        across_both = product(parts(upper), lower, across)
        put(outs[:2], product(lower, parts(across_both), plain))
        put(outs[2:4], across_both)

    hand_on(ins[n if section else 2 :], outs[4:])


def combine_body(last, spans, ins, outs):
    pairs, node = ins[: 2 * len(spans)], ins[2 * len(spans) :]

    def rows_of(refs):
        return jnp.concatenate([ref[at : at + width] for ref, (at, width) in zip(refs, spans)])

    mine, other = rows_of(pairs[::2]), rows_of(pairs[1::2])
    by_mine = node[0][...], node[1][...]
    by_other = node[2][...], node[3][...]
    change = product(parts(mine), by_mine, plain) + product(parts(other), by_other, plain)
    result = mine - change
    outs[0][...] = result.T if last else result


def cut(columns, width, ahead=()):
    widths = []
    left = columns
    for each in list(ahead) + [width] * (columns // width):
        if each <= left:
            widths.append(each)
            left -= each
    return widths + [left] * (left > 0)


def spans_of(widths):
    return [(sum(widths[:i]), width) for i, width in enumerate(widths)]


def cuts_of(columns, levels):
    if columns % LANES:
        return [[(0, columns)]] * (levels + 1)
    double = min(columns, 2 * LANES)
    coarse = spans_of(cut(columns, double))
    fine = spans_of(cut(columns, double, (LANES, LANES)))
    first = spans_of(cut(columns, max(columns - double, LANES), (double,)))
    return [first] + [fine] * (levels - 2) + [coarse] * (min(levels, 2))


def order_of(cuts):
    order = []
    for s, given in enumerate(cuts[1:]):
        for c, (start, _) in enumerate(given):
            wave = max(i for i, (at, _) in enumerate(cuts[-1]) if at <= start)
            order.append((s + wave, s, c))
    return [at[1:] for at in sorted(order)]


def per_device(trailing, reflectors, leaf_factor, node_reflect, node_factor):
    line = Line()
    rows, columns = trailing.shape
    size, piece = leaf_factor.shape
    levels = node_factor.shape[0]
    cuts = cuts_of(columns, levels)
    early = cuts[0][0][1]
    copied = pl.BlockSpec(memory_space=pltpu.VMEM)
    far_away = pl.BlockSpec(memory_space=pl.ANY)

    vectors = col_blocks(reflectors)
    n = len(vectors)
    factor = col_blocks(leaf_factor)
    pieces = line(
        functools.partial(pick_body, levels),
        "pick",
        [(in_hbm(x), far_away) for x in (node_reflect, node_factor)],
        [held(size, piece)] * levels,
        scratch=[pltpu.SemaphoreType.DMA((levels,))],
    )
    far = [None] + [swapped(pieces[s], "row", s) for s in range(1, levels)]

    def stacked(sections):
        given = [x for s in sections for x in (pieces[s], far[s])]
        return given, [held(2 * size, piece)] * len(sections)

    vec_h, vec_l, vect_h, vect_l, inn_h, inn_l, zeroth = line(
        functools.partial(inner_body, n),
        "inner",
        [(vectors[0], copied)] + vectors[1:] + [trailing, pieces[0]],
        held_parts(rows, size)
        + held_parts(size, rows)
        + held_parts(size, early)
        + [held(size, piece)],
    )
    zeroth = col_blocks(zeroth)
    sources = [(inn_h, inn_l)]
    if columns > early:
        sources.append(
            line(
                functools.partial(later_body, early),
                "later",
                [vect_h, vect_l, trailing],
                held_parts(size, columns - early),
            )
        )
    top, high, low, tri_h, tri_l = line(
        functools.partial(first_body, n),
        "first",
        [inn_h, inn_l, vec_h, vec_l, trailing] + [(factor[0], copied)] + factor[1:],
        [held(early, size)] + held_parts(size, early) + held_parts(size, size),
    )
    tops = [[(0, early, top, swapped(top, "row", 0))]] + [[] for _ in range(levels)]
    scaled = [high, low]
    nodes = [None] * levels
    out = None

    stacks = [None] * levels
    if columns > early:
        given, made = stacked(range(1, min(levels, 3)))
        width = columns - early
        top, high, low, *stacks[1:3] = line(
            functools.partial(tops_body, early, 0),
            "tops",
            list(sources[1]) + [vec_h, vec_l, trailing, tri_h, tri_l] + given,
            [held(width, size)] + held_parts(size, width) + made,
        )
        scaled += [high, low]
        tops[0].append((early, width, top, swapped(top, "row", 0)))
    elif levels > 1:
        stacks[1:3] = line(hand_on, "hand", *stacked(range(1, min(levels, 3))))
    given, made = stacked(range(3, levels))
    own, *stacks[3:] = line(
        functools.partial(join_body, n), "join", zeroth + given, [held(size, size)] + made
    )
    partner = swapped(own, "row", 0)
    (other,) = line(hand_on, "hand", [tops[0][0][3]], [held(early, size)])
    tops[0][0] = *tops[0][0][:3], other

    def node_of(s):
        inputs = [own, partner]
        if s:
            inputs = col_blocks(stacks[s])
        held_back = [t for t in range(3, levels) if s == t - 1]
        *nodes[s], = line(
            functools.partial(node_body, s, n),
            "node",
            inputs + [stacks[t] for t in held_back],
            held_parts(size, size) * 2 + [held(2 * size, piece)] * len(held_back),
        )
        for t in held_back:
            stacks[t] = nodes[s].pop()

    for s, c in order_of(cuts):
        if nodes[s] is None:
            if 2 < s == levels - 1:
                at, extent, mine, other = tops[s][0]
                (other,) = line(hand_on, "hand", [other], [held(*other.shape)])
                tops[s][0] = at, extent, mine, other
            node_of(s)
        start, width = cuts[s + 1][c]
        inputs, spans = [], []
        for at, extent, mine, other in tops[s]:
            low, high = max(at, start), min(at + extent, start + width)
            if low < high:
                if low > start:
                    inputs[1::2] = line(
                        hand_on, "hand", inputs[1::2], [held(*x.shape) for x in inputs[1::2]]
                    )
                inputs += [mine, other]
                spans.append((low - at, high - low))
        inputs += nodes[s]
        last = s == levels - 1
        body = functools.partial(combine_body, last, spans)
        if not last:
            (top,) = line(body, "combine", inputs, [held(width, size)])
            tops[s + 1].append((start, width, top, swapped(top, "row", s + 1)))
            if levels > 2 and (s, c) == (0, min(2, len(cuts[1]) - 1)):
                (stacks[2],) = line(hand_on, "hand", [stacks[2]], [held(2 * size, piece)])
        else:
            if out is None:
                (out,) = line(
                    rest_body,
                    "rest",
                    [trailing, vec_h, vec_l] + scaled,
                    [
                        (
                            jax.ShapeDtypeStruct((rows, columns), f32),
                            pl.BlockSpec(
                                (pl.Element(rows - size), pl.Element(columns)), lambda i: (size, 0)
                            ),
                        )
                    ],
                )
            block = pl.BlockSpec(
                (pl.Element(size), pl.Element(width)), lambda i, start=start: (0, start)
            )
            (out,) = line(
                body,
                "finish",
                inputs,
                [(jax.ShapeDtypeStruct((rows, columns), f32), block)],
                alias=(out, 0),
            )
    return out


def solution(mesh):
    in_specs = (
        P("row", "col"),
        P("row", "col"),
        P("row", "col"),
        P(None, "row", "col"),
        P(None, "row", "col"),
    )
    out_specs = P("row", "col")
    return jax.shard_map(
        per_device, mesh=mesh, in_specs=in_specs, out_specs=out_specs, check_vma=False
    )
```

```python
import functools

import jax
import jax.numpy as jnp
from jax import lax
from jax.experimental import pallas as pl
from jax.experimental.pallas import tpu as pltpu
from jax.sharding import PartitionSpec as P

f32 = jnp.float32
bf16 = jnp.bfloat16
LANES = 128
VMEM_LIMIT = 32 * 2**20
USUAL = dict(
    pick=11.0,
    inner=10.0,
    later=24.0,
    first=6.0,
    tops=10.0,
    hand=1.0,
    join=1.0,
    node=1.5,
    combine=6.0,
    rest=17.0,
    finish=13.0,
)


def swapped(value, axis, apart):
    mask = 2**apart
    pairs = [(source, source ^ mask) for source in range(lax.axis_size(axis))]
    return lax.ppermute(value, axis, pairs)


def turned(value, axis):
    size = lax.axis_size(axis)
    return [
        lax.ppermute(value, axis, [((to + step) % size, to) for to in range(size)])
        for step in range(1, size)
    ]


def col_blocks(value):
    if value.shape[-1] % LANES == 0:
        return [value] + turned(value, "col")
    return [lax.all_gather(value, "col", axis=value.ndim - 1, tiled=True)]


def whole(blocks):
    if len(blocks) == 1:
        return blocks[0]
    size = len(blocks)
    me = lax.axis_index("col")
    ordered = []
    for at in range(size):
        block = blocks[0]
        for step in range(1, size):
            block = jnp.where((me + step) % size == at, blocks[step], block)
        ordered.append(block)
    return jnp.concatenate(ordered, axis=1)


def triangle(factor):
    row = lax.broadcasted_iota(jnp.int32, factor.shape, 0)
    column = lax.broadcasted_iota(jnp.int32, factor.shape, 1)
    kept = jnp.where(row <= column, factor, 0.0)
    return kept + jnp.where(row == column, 0.5, 0.0)


def parts(value):
    high = value.astype(bf16)
    return high, (value - high.astype(f32)).astype(bf16)


def put(refs, value, at=...):
    for ref, part in zip(refs, parts(value)):
        ref[at] = part


def product(left, right, over):
    def dot(a, b):
        return lax.dot_general(a, b, (over, ((), ())), preferred_element_type=f32)

    rows = left[0].shape[0]
    both = dot(jnp.concatenate(left), right[0])
    return both[:rows] + (dot(left[0], right[1]) + both[rows:])


plain = ((1,), (0,))
across = ((1,), (1,))


class Line:
    def __init__(self):
        self.token = None

    def __call__(self, body, name, inputs, outputs, grid=(1,), alias=None, scratch=()):
        operands, in_specs = [], []
        for value in inputs:
            if isinstance(value, tuple):
                operands.append(value[0])
                in_specs.append(value[1])
            else:
                operands.append(pltpu.with_memory_space_constraint(value, pltpu.VMEM))
                in_specs.append(pl.BlockSpec(memory_space=pltpu.VMEM))
        n_in = len(operands)
        if self.token is not None:
            operands.append(pltpu.with_memory_space_constraint(self.token, pltpu.VMEM))
            in_specs.append(pl.BlockSpec(memory_space=pltpu.VMEM))
        aliases = {}
        if alias is not None:
            aliases = {len(operands): alias[1]}
            operands.append(alias[0])
            in_specs.append(pl.BlockSpec(memory_space=pl.ANY))
        out_shape, out_specs = [], []
        for shape, spec in outputs:
            out_shape.append(shape)
            out_specs.append(spec)
        out_shape.append(pltpu.VMEM((8, LANES), f32))
        out_specs.append(pl.BlockSpec(memory_space=pltpu.VMEM))
        n_all = len(operands)
        at_token = n_all + len(outputs)

        def kernel(*refs):
            refs[at_token][...] = jnp.zeros((8, LANES), f32)
            body(refs[:n_in], refs[n_all:at_token] + refs[at_token + 1 :])

        *results, self.token = pl.pallas_call(
            kernel,
            grid=grid,
            out_shape=out_shape,
            in_specs=in_specs,
            out_specs=out_specs,
            scratch_shapes=scratch,
            input_output_aliases=aliases,
            compiler_params=pltpu.CompilerParams(vmem_limit_bytes=VMEM_LIMIT),
            cost_estimate=pl.CostEstimate(
                flops=int(USUAL[name] * 1.15e9), bytes_accessed=0, transcendentals=0
            ),
            name=name,
        )(*operands)
        return results


def in_hbm(value):
    return pltpu.with_memory_space_constraint(value, pltpu.HBM)


def held(*shape, dtype=f32):
    return pltpu.VMEM(shape, dtype), pl.BlockSpec(memory_space=pltpu.VMEM)


def held_parts(*shape):
    return [held(*shape, dtype=bf16)] * 2


def pick_body(levels, ins, outs):
    reflect, factor, sems = ins[0], ins[1], outs[levels]
    position = lax.axis_index("row")
    for s in range(levels):
        clear = position // (1 << s) % 2 == 0

        @pl.when(clear)
        def _(s=s):
            pltpu.make_async_copy(factor.at[s], outs[s], sems.at[s]).start()

        @pl.when(jnp.logical_not(clear))
        def _(s=s):
            pltpu.make_async_copy(reflect.at[s], outs[s], sems.at[s]).start()

    for s in range(levels):
        pltpu.make_async_copy(factor.at[s], outs[s], sems.at[s]).wait()


def inner_body(n, ins, outs):
    trailing = ins[n]
    full = whole([ref[...] for ref in ins[:n]])
    put(outs[:2], full)
    turned_parts = parts(full.T)
    for ref, part in zip(outs[2:4], turned_parts):
        ref[...] = part
    width = outs[4].shape[1]
    put(outs[4:6], product(turned_parts, parts(trailing[:, :width]), plain))
    outs[6][...] = ins[n + 1][...]


def later_body(start, ins, outs):
    trailing = ins[2][:, start:]
    put(outs[:2], product((ins[0][...], ins[1][...]), parts(trailing), plain))


def first_body(n, ins, outs):
    put(outs[3:5], triangle(whole([ref[...] for ref in ins[5 : 5 + n]])).T)
    tops_body(0, 0, list(ins[:5]) + list(outs[3:5]), outs[:3])


def join_body(n, ins, outs):
    outs[0][...] = whole([ref[...] for ref in ins[:n]])
    hand_on(ins[n:], outs[1:])


def tops_body(start, inner_start, ins, outs):
    inn_h, inn_l, vec_h, vec_l, trailing, tri_h, tri_l = ins[:7]
    width, size = outs[0].shape
    at = slice(inner_start, inner_start + width)
    scaled = parts(product((tri_h[...], tri_l[...]), (inn_h[:, at], inn_l[:, at]), plain))
    outs[1][...] = scaled[0]
    outs[2][...] = scaled[1]
    taken = product((vec_h[:size], vec_l[:size]), scaled, plain)
    outs[0][...] = (trailing[:size, start : start + width] - taken).T
    hand_on(ins[7:], outs[3:])


def rest_body(ins, outs):
    trailing, vec_h, vec_l = ins[:3]
    size = vec_h.shape[1]
    pieces = ins[3:]
    start = 0
    for high, low in zip(pieces[::2], pieces[1::2]):
        width = high.shape[1]
        at = slice(start, start + width)
        taken = product((vec_h[size:], vec_l[size:]), (high[...], low[...]), plain)
        outs[0][:, at] = trailing[size:, at] - taken
        start += width


def hand_on(ins, outs):
    ins = list(ins)
    for out in outs:
        at = 0
        while at < out.shape[0]:
            piece = ins.pop(0)
            out[at : at + piece.shape[0]] = piece[...]
            at += piece.shape[0]


def node_body(section, n, ins, outs):
    clear = lax.axis_index("row") // (1 << section) % 2 == 0
    size = outs[0].shape[0]
    if section == 0:
        own, partner = ins[0][...], ins[1][...]
    else:
        own = whole([ref[:size] for ref in ins[:n]])
        partner = whole([ref[size:] for ref in ins[:n]])
    lower = parts(jnp.where(clear, partner, own))
    upper = triangle(jnp.where(clear, own, partner))

    @pl.when(clear)
    def _():
        put(outs[:2], upper)
        put(outs[2:4], product(lower, parts(upper), plain))

    @pl.when(jnp.logical_not(clear))
    def _():
        across_both = product(parts(upper), lower, across)
        put(outs[:2], product(lower, parts(across_both), plain))
        put(outs[2:4], across_both)

    hand_on(ins[n if section else 2 :], outs[4:])


def combine_body(last, spans, ins, outs):
    pairs, node = ins[: 2 * len(spans)], ins[2 * len(spans) :]

    def rows_of(refs):
        return jnp.concatenate([ref[at : at + width] for ref, (at, width) in zip(refs, spans)])

    mine, other = rows_of(pairs[::2]), rows_of(pairs[1::2])
    by_mine = node[0][...], node[1][...]
    by_other = node[2][...], node[3][...]
    change = product(parts(mine), by_mine, plain) + product(parts(other), by_other, plain)
    result = mine - change
    outs[0][...] = result.T if last else result


def cut(columns, width, ahead=()):
    widths = []
    left = columns
    for each in list(ahead) + [width] * (columns // width):
        if each <= left:
            widths.append(each)
            left -= each
    return widths + [left] * (left > 0)


def spans_of(widths):
    return [(sum(widths[:i]), width) for i, width in enumerate(widths)]


def cuts_of(columns, levels):
    if columns % LANES:
        return [[(0, columns)]] * (levels + 1)
    double = min(columns, 2 * LANES)
    coarse = spans_of(cut(columns, double))
    fine = spans_of(cut(columns, double, (LANES, LANES)))
    first = spans_of(cut(columns, max(columns - double, LANES), (double,)))
    return [first] + [fine] * (levels - 2) + [coarse] * (min(levels, 2))


def order_of(cuts):
    order = []
    for s, given in enumerate(cuts[1:]):
        for c, (start, _) in enumerate(given):
            wave = max(i for i, (at, _) in enumerate(cuts[-1]) if at <= start)
            order.append((s + wave, s, c))
    return [at[1:] for at in sorted(order)]


def per_device(trailing, reflectors, leaf_factor, node_reflect, node_factor):
    line = Line()
    rows, columns = trailing.shape
    size, piece = leaf_factor.shape
    levels = node_factor.shape[0]
    cuts = cuts_of(columns, levels)
    early = cuts[0][0][1]
    copied = pl.BlockSpec(memory_space=pltpu.VMEM)
    far_away = pl.BlockSpec(memory_space=pl.ANY)

    vectors = col_blocks(reflectors)
    n = len(vectors)
    factor = col_blocks(leaf_factor)
    pieces = line(
        functools.partial(pick_body, levels),
        "pick",
        [(in_hbm(x), far_away) for x in (node_reflect, node_factor)],
        [held(size, piece)] * levels,
        scratch=[pltpu.SemaphoreType.DMA((levels,))],
    )
    far = [None] + [swapped(pieces[s], "row", s) for s in range(1, levels)]

    def stacked(sections):
        given = [x for s in sections for x in (pieces[s], far[s])]
        return given, [held(2 * size, piece)] * len(sections)

    vec_h, vec_l, vect_h, vect_l, inn_h, inn_l, zeroth = line(
        functools.partial(inner_body, n),
        "inner",
        [(vectors[0], copied)] + vectors[1:] + [trailing, pieces[0]],
        held_parts(rows, size)
        + held_parts(size, rows)
        + held_parts(size, early)
        + [held(size, piece)],
    )
    zeroth = col_blocks(zeroth)
    sources = [(inn_h, inn_l)]
    if columns > early:
        sources.append(
            line(
                functools.partial(later_body, early),
                "later",
                [vect_h, vect_l, trailing],
                held_parts(size, columns - early),
            )
        )
    top, high, low, tri_h, tri_l = line(
        functools.partial(first_body, n),
        "first",
        [inn_h, inn_l, vec_h, vec_l, trailing] + [(factor[0], copied)] + factor[1:],
        [held(early, size)] + held_parts(size, early) + held_parts(size, size),
    )
    tops = [[(0, early, top, swapped(top, "row", 0))]] + [[] for _ in range(levels)]
    scaled = [high, low]
    nodes = [None] * levels
    out = None

    stacks = [None] * levels
    if columns > early:
        given, made = stacked(range(1, min(levels, 3)))
        width = columns - early
        top, high, low, *stacks[1:3] = line(
            functools.partial(tops_body, early, 0),
            "tops",
            list(sources[1]) + [vec_h, vec_l, trailing, tri_h, tri_l] + given,
            [held(width, size)] + held_parts(size, width) + made,
        )
        scaled += [high, low]
        tops[0].append((early, width, top, swapped(top, "row", 0)))
    elif levels > 1:
        stacks[1:3] = line(hand_on, "hand", *stacked(range(1, min(levels, 3))))
    given, made = stacked(range(3, levels))
    own, *stacks[3:] = line(
        functools.partial(join_body, n), "join", zeroth + given, [held(size, size)] + made
    )
    partner = swapped(own, "row", 0)
    (other,) = line(hand_on, "hand", [tops[0][0][3]], [held(early, size)])
    tops[0][0] = *tops[0][0][:3], other

    def node_of(s):
        inputs = [own, partner]
        if s:
            inputs = col_blocks(stacks[s])
        held_back = [t for t in range(3, levels) if s == t - 1]
        *nodes[s], = line(
            functools.partial(node_body, s, n),
            "node",
            inputs + [stacks[t] for t in held_back],
            held_parts(size, size) * 2 + [held(2 * size, piece)] * len(held_back),
        )
        for t in held_back:
            stacks[t] = nodes[s].pop()

    for s, c in order_of(cuts):
        if nodes[s] is None:
            if 2 < s == levels - 1:
                at, extent, mine, other = tops[s][0]
                (other,) = line(hand_on, "hand", [other], [held(*other.shape)])
                tops[s][0] = at, extent, mine, other
            node_of(s)
        start, width = cuts[s + 1][c]
        inputs, spans = [], []
        for at, extent, mine, other in tops[s]:
            low, high = max(at, start), min(at + extent, start + width)
            if low < high:
                if low > start:
                    inputs[1::2] = line(
                        hand_on, "hand", inputs[1::2], [held(*x.shape) for x in inputs[1::2]]
                    )
                inputs += [mine, other]
                spans.append((low - at, high - low))
        inputs += nodes[s]
        last = s == levels - 1
        body = functools.partial(combine_body, last, spans)
        if not last:
            (top,) = line(body, "combine", inputs, [held(width, size)])
            tops[s + 1].append((start, width, top, swapped(top, "row", s + 1)))
            if levels > 2 and (s, c) == (1, 0):
                (stacks[2],) = line(hand_on, "hand", [stacks[2]], [held(2 * size, piece)])
        else:
            if out is None:
                (out,) = line(
                    rest_body,
                    "rest",
                    [trailing, vec_h, vec_l] + scaled,
                    [
                        (
                            jax.ShapeDtypeStruct((rows, columns), f32),
                            pl.BlockSpec(
                                (pl.Element(rows - size), pl.Element(columns)), lambda i: (size, 0)
                            ),
                        )
                    ],
                )
            block = pl.BlockSpec(
                (pl.Element(size), pl.Element(width)), lambda i, start=start: (0, start)
            )
            (out,) = line(
                body,
                "finish",
                inputs,
                [(jax.ShapeDtypeStruct((rows, columns), f32), block)],
                alias=(out, 0),
            )
    return out


def solution(mesh):
    in_specs = (
        P("row", "col"),
        P("row", "col"),
        P("row", "col"),
        P(None, "row", "col"),
        P(None, "row", "col"),
    )
    out_specs = P("row", "col")
    return jax.shard_map(
        per_device, mesh=mesh, in_specs=in_specs, out_specs=out_specs, check_vma=False
    )
```
